32 devices in a mesh: groups: 2 (over y), train: 4 (over z), test: 2 (over x), proj: 2 (over core).
Axes of the slice: x: 2, y: 2, z: 4, core: 2. Of those that a mesh axis runs over, the one named last changes fastest.
Arguments:
- train_acts: bfloat16 [16, 128, 4096], P(('groups', 'train', 'test'), None, 'proj'), parts along dimension 0, may hold values from -6 to 6
- train_grads: bfloat16 [16, 128, 14336], P(('groups', 'train', 'test'), None, 'proj'), parts along dimension 0, may hold values from -6 to 6
- train_segs: int32 [16, 128], P(('groups', 'train', 'test')), parts along dimension 0, may hold values from 0 to 7, never falling along the last dimension, each value on 1 to 24 neighbouring positions
- train_mask: int32 [16, 128], P(('groups', 'train', 'test')), parts along dimension 0, may hold values 0 or 1
- test_acts: bfloat16 [16, 64, 4096], P(('groups', 'train', 'test'), None, 'proj'), parts along dimension 0, may hold values from -6 to 6
- test_grads: bfloat16 [16, 64, 14336], P(('groups', 'train', 'test'), None, 'proj'), parts along dimension 0, may hold values from -6 to 6
- test_segs: int32 [16, 64], P(('groups', 'train', 'test')), parts along dimension 0, may hold values from 0 to 3, never falling along the last dimension, each value on 1 to 24 neighbouring positions
- test_mask: int32 [16, 64], P(('groups', 'train', 'test')), parts along dimension 0, may hold values 0 or 1
- proj_in: bfloat16 [4096, 32], P('proj'), may hold values from -0.09375 to 0.09375
- proj_out: bfloat16 [14336, 32], P('proj'), may hold values from -0.046875 to 0.046875
Outputs:
- scores: float32 [128, 32], P(('groups', 'train', 'test'), 'proj'), parts along dimension 0
The draws below stay inside these ranges and needn't reach their ends.
There are 2 independent parts, one for each index of `groups`. The reference program is written for one: setup_inputs(seed, part) draws one part's arguments, and reference() takes and returns one part's arrays. A program takes and returns all parts, laid end to end along the dimension named above; an argument that names none is the same for every part. Nothing has to cross between parts.
Inputs may be any that keep to these rules, and one draw needn't show every extreme that they name: `train_segs`: within each shard's row the example numbers never fall and every number 0 to 7 names 1 to 24 tokens. `test_segs`: within each shard's row the example numbers never fall and every number 0 to 3 names 1 to 24 tokens.
All inputs are finite; a program needn't handle non-finite values. No bound on the sum of `train_mask` or of `test_mask` on one device may be relied on, other than what follows from the above.
Results may differ from the reference program's by a relative error of at most 0.0003.
Values sent between devices are 32-bit elements; how exact they have to be, the bound alone decides.
No kernel may reach another device: no remote copies, remote signals or barrier semaphores. Data moves between devices by JAX's collectives and lax.ppermute only.
A program may use at most 64 MiB of HBM per device.

```python
import math
import jax
import jax.numpy as jnp
import numpy as np
from jax import lax

D = 4096
FF = 14336
RIN = 32
ROUT = 32
SEGMAX = 24
TOK_DEV = 128
TTOK_DEV = 64
EX_DEV = 8
TEX_DEV = 4
SHARDS = 8
TRAIN_EX = 64


def plant(array, key, least, top_value):
    longest = array.shape.index(max(array.shape))
    spots = []
    for shift in (0, 1):
        where = [jax.random.randint(jax.random.fold_in(key, axis), (), 0, length) for axis, length in enumerate(array.shape)]
        where[longest] = (where[longest] + shift) % array.shape[longest]
        spots.append(tuple(where))
    return array.at[spots[0]].set(least).at[spots[1]].set(top_value)


def steps_of(rng, dims, cuts, low, top_value):
    factor_of, own = 1.0, jax.random.fold_in(rng, 6)
    for position, blocks in cuts:
        draws = jnp.exp(jax.random.uniform(jax.random.fold_in(own, position), (blocks,), jnp.float32, low / len(cuts), top_value / len(cuts)))
        factor_of = factor_of * jnp.repeat(draws, dims[position] // blocks).reshape([-1 if axis == position else 1 for axis in range(len(dims))])
    return factor_of


def length_profile(number_of, total, bound, slope):
    loads = [(1 << 20) // math.isqrt(standing ** slope) + 1 for standing in range(2, number_of + 1)]
    rest, holding = total - bound - (number_of - 1), [1] * (number_of - 1)
    while rest > 0:
        movable = [i for i in range(number_of - 1) if holding[i] < bound]
        pool, left = sum([loads[i] for i in movable]), rest
        for i in movable:
            extra = min(bound - holding[i], max(1, left * loads[i] // pool), rest)
            holding[i] = holding[i] + extra
            rest = rest - extra
    return np.array([bound] + holding)


def ragged_sizes(rng, number_of, total, limit, skew):
    if number_of == 2:
        one = jax.random.randint(rng, (), max(1, total - limit), min(limit, total - 1) + 1)
        return jnp.stack([one, total - one])
    lengths = jnp.asarray(length_profile(number_of, total, limit, skew), jnp.int32)
    pairs = (number_of - 1) // 2
    donor, taker = lengths[1:1 + 2 * pairs:2], lengths[2:2 + 2 * pairs:2]
    slack = jnp.minimum(donor - 1, limit - taker)
    shifted = jax.random.randint(jax.random.fold_in(rng, 1), (pairs,), 0, 1 << 20) % (slack + 1)
    lengths = lengths.at[1:1 + 2 * pairs:2].set(donor - shifted).at[2:2 + 2 * pairs:2].set(taker + shifted)
    return lengths[jax.random.permutation(jax.random.fold_in(rng, 2), number_of)]


def normal_values(key, shape, spread, limit, cuts=(), kind=jnp.bfloat16):
    result = jax.random.normal(key, shape, jnp.float32) * spread
    if len(cuts) > 0:
        result = steps_of(key, shape, cuts, -0.22, 0.18) * result
    return jnp.clip(result, min=-limit, max=limit).astype(kind)


def setup_inputs(seed: int = 0, part: int = 0) -> dict:
    streams_of = jax.random.split(jax.random.key(seed), 11)
    part_splits = jax.random.split(jax.random.fold_in(streams_of[10], part), 11)
    return {
        "train_acts": normal_values(part_splits[0], (SHARDS, TOK_DEV, D), 1.0, 6.0, ((0, 8), (2, 2))),
        "train_grads": normal_values(part_splits[1], (SHARDS, TOK_DEV, FF), 1.0, 6.0, ((0, 8), (2, 2))),
        "train_segs": jax.vmap(lambda own: jnp.searchsorted(jnp.cumsum(ragged_sizes(own, EX_DEV, TOK_DEV, SEGMAX, 1)), jnp.arange(TOK_DEV), side="right"))(jax.random.split(part_splits[2], SHARDS)).reshape((SHARDS, TOK_DEV)).astype(jnp.int32),
        "train_mask": plant((jax.random.randint(part_splits[3], (SHARDS, TOK_DEV), 0, 8) < 7).astype(jnp.int32), jax.random.fold_in(part_splits[3], 1), 0, 1),
        "test_acts": normal_values(part_splits[4], (SHARDS, TTOK_DEV, D), 1.0, 6.0, ((0, 8), (2, 2))),
        "test_grads": normal_values(part_splits[5], (SHARDS, TTOK_DEV, FF), 1.0, 6.0, ((0, 8), (2, 2))),
        "test_segs": jax.vmap(lambda own: jnp.searchsorted(jnp.cumsum(ragged_sizes(own, TEX_DEV, TTOK_DEV, SEGMAX, 1)), jnp.arange(TTOK_DEV), side="right"))(jax.random.split(part_splits[6], SHARDS)).reshape((SHARDS, TTOK_DEV)).astype(jnp.int32),
        "test_mask": plant((jax.random.randint(part_splits[7], (SHARDS, TTOK_DEV), 0, 8) < 7).astype(jnp.int32), jax.random.fold_in(part_splits[7], 1), 0, 1),
        "proj_in": normal_values(streams_of[8], (D, RIN), D ** -0.5, 0.09375, ((0, 2),)),
        "proj_out": normal_values(streams_of[9], (FF, ROUT), FF ** -0.5, 0.046875, ((0, 2),)),
    }


def example_grads(acts, grads, segs, mask, proj_in, proj_out, count):
    shards, tokens = (acts.shape[0], acts.shape[1])
    xp = jnp.dot(acts.reshape(shards * tokens, -1).astype(jnp.float32), proj_in.astype(jnp.float32), preferred_element_type=jnp.float32)
    gp = jnp.dot(grads.reshape(shards * tokens, -1).astype(jnp.float32), proj_out.astype(jnp.float32), preferred_element_type=jnp.float32)
    xp = xp * mask.reshape(-1, 1).astype(jnp.float32)
    outer = (xp[:, :, None] * gp[:, None, :]).reshape(shards, tokens, -1)
    onehot = (segs[:, :, None] == jnp.arange(count, dtype=jnp.int32)[None, None, :]).astype(jnp.float32)
    summed = jnp.einsum('ste,stk->sek', onehot, outer, precision=lax.Precision.HIGHEST)
    return summed.reshape(shards * count, -1)

def reference(train_acts, train_grads, train_segs, train_mask, test_acts, test_grads, test_segs, test_mask, proj_in, proj_out):
    train_g = example_grads(train_acts, train_grads, train_segs, train_mask, proj_in, proj_out, EX_DEV)
    test_g = example_grads(test_acts, test_grads, test_segs, test_mask, proj_in, proj_out, TEX_DEV)
    width = train_g.shape[1]
    hessian = jnp.dot(train_g.T, train_g, precision=lax.Precision.HIGHEST) / TRAIN_EX + jnp.eye(width, dtype=jnp.float32)
    factor = jnp.linalg.cholesky(hessian)
    solved = jax.scipy.linalg.cho_solve((factor, True), test_g.T)
    return jnp.dot(train_g, solved, precision=lax.Precision.HIGHEST) / jnp.sqrt(jnp.float32(width))
```

```python
import jax
import jax.numpy as jnp
from jax import lax
from jax.sharding import PartitionSpec as P

EX_DEV = 8
TEX_DEV = 4


def per_example(xp, gp, segs, mask, count):
    xp = xp * mask.reshape(-1, 1).astype(jnp.float32)
    outer = (xp[:, :, None] * gp[:, None, :]).reshape(xp.shape[0], -1)
    onehot = (jnp.arange(count, dtype=jnp.int32)[:, None] == segs).astype(jnp.float32)
    return jnp.dot(onehot, outer, precision=lax.Precision.HIGHEST)


def body(
    train_acts,
    train_grads,
    train_segs,
    train_mask,
    test_acts,
    test_grads,
    test_segs,
    test_mask,
    proj_in,
    proj_out,
):

    def project(acts, grads):
        rows = acts.shape[0] * acts.shape[1]
        xp = jnp.dot(acts.reshape(rows, -1), proj_in, preferred_element_type=jnp.float32)
        gp = jnp.dot(grads.reshape(rows, -1), proj_out, preferred_element_type=jnp.float32)
        return (xp, gp)

    train_xp, train_gp = project(train_acts, train_grads)
    test_xp, test_gp = project(test_acts, test_grads)
    train_xp, train_gp, test_xp, test_gp = lax.psum((train_xp, train_gp, test_xp, test_gp), "proj")
    train_own = per_example(train_xp, train_gp, train_segs, train_mask, EX_DEV)
    test_own = per_example(test_xp, test_gp, test_segs, test_mask, TEX_DEV)
    width = train_own.shape[1]
    shards = lax.axis_size(("train", "test"))
    total_ex = EX_DEV * shards
    total_tex = TEX_DEV * shards
    both = lax.all_gather(jnp.concatenate([train_own, test_own], 0), ("train", "test"), axis=0)
    train_full = both[:, :EX_DEV].reshape(total_ex, width)
    test_full = both[:, EX_DEV:].reshape(total_tex, width)
    cols = total_tex // lax.axis_size("proj")
    test_half = lax.dynamic_slice_in_dim(test_full, lax.axis_index("proj") * cols, cols, 0)
    gram = jnp.dot(train_full, train_full.T, precision=lax.Precision.HIGHEST)
    cross = jnp.dot(train_full, test_half.T, precision=lax.Precision.HIGHEST)
    system = gram / total_ex + jnp.eye(total_ex, dtype=jnp.float32)
    factor = jnp.linalg.cholesky(system)
    solved = jax.scipy.linalg.cho_solve((factor, True), cross)
    scale = 1.0 / jnp.sqrt(jnp.float32(width))
    row = lax.axis_index(("train", "test")) * EX_DEV
    return lax.dynamic_slice_in_dim(solved, row, EX_DEV, 0) * scale


def solution(mesh):
    return jax.shard_map(
        body,
        mesh=mesh,
        in_specs=(
            P(("groups", "train", "test"), None, "proj"),
            P(("groups", "train", "test"), None, "proj"),
            P(("groups", "train", "test"), None),
            P(("groups", "train", "test"), None),
            P(("groups", "train", "test"), None, "proj"),
            P(("groups", "train", "test"), None, "proj"),
            P(("groups", "train", "test"), None),
            P(("groups", "train", "test"), None),
            P("proj", None),
            P("proj", None),
        ),
        out_specs=P(("groups", "train", "test"), "proj"),
        check_vma=False,
    )
```

```python
import functools

import jax
import jax.numpy as jnp
from jax import lax
from jax.experimental import pallas as pl
from jax.experimental.pallas import tpu as pltpu
from jax.sharding import PartitionSpec as P

EX_DEV = 8
TEX_DEV = 4
ROWS = 16
F32 = jnp.float32
BF16 = jnp.bfloat16
NT = (((1,), (1,)), ((), ()))
NN = (((1,), (0,)), ((), ()))
VMEM = pl.BlockSpec(memory_space=pltpu.VMEM)
SMEM = pl.BlockSpec(memory_space=pltpu.SMEM)
HBM = pl.BlockSpec(memory_space=pltpu.HBM)


def split(x):
    hi = x.astype(BF16)
    rest = x - hi.astype(F32)
    mid = rest.astype(BF16)
    low = (rest - mid.astype(F32)).astype(BF16)
    return hi, mid, low


def mm(a, b, dims):
    return lax.dot_general(a, b, dims, preferred_element_type=F32)


def chunks_of(total, parts):
    size = total // parts
    return [(n * size, size) for n in range(parts)]


def project_kernel(ta, tg, sa, sg, pin, pout, out, acts, grads, win, wout, sems):
    rows = ta.shape[0]
    both = acts.shape[0]
    copies = []

    def copy(src, dst):
        dma = pltpu.make_async_copy(src, dst, sems.at[len(copies)])
        dma.start()
        copies.append(dma)
        return dma

    first = [
        copy(pin, win),
        copy(ta, acts.at[pl.ds(0, rows)]),
        copy(sa, acts.at[pl.ds(rows, both - rows)]),
        copy(pout, wout),
    ]
    later = []
    for start, size in chunks_of(grads.shape[1], 4):
        cols = pl.ds(start, size)
        later.append(
            (
                copy(tg.at[:, cols], grads.at[pl.ds(0, rows), cols]),
                copy(sg.at[:, cols], grads.at[pl.ds(rows, both - rows), cols]),
                start,
                size,
            )
        )
    for dma in first[:3]:
        dma.wait()
    xp = mm(acts[...], win[...], NT)
    first[3].wait()
    gp = None
    for one, two, start, size in later:
        one.wait()
        two.wait()
        cols = slice(start, start + size)
        part = mm(grads[:, cols], wout[:, cols], NT)
        gp = part if gp is None else gp + part
    rin = xp.shape[1]
    out[:, :rin] = xp
    out[:, rin:] = gp


def project(ta, tg, sa, sg, pin, pout):
    both = ta.shape[0] + sa.shape[0]
    rin, rout = pin.shape[0], pout.shape[0]
    return pl.pallas_call(
        project_kernel,
        out_shape=jax.ShapeDtypeStruct((both, rin + rout), F32),
        in_specs=[HBM] * 6,
        out_specs=VMEM,
        scratch_shapes=[
            pltpu.VMEM((both, ta.shape[1]), BF16),
            pltpu.VMEM((both, tg.shape[1]), BF16),
            pltpu.VMEM(pin.shape, BF16),
            pltpu.VMEM(pout.shape, BF16),
            pltpu.SemaphoreType.DMA((12,)),
        ],
        compiler_params=pltpu.CompilerParams(vmem_limit_bytes=60 << 20),
        name="project",
    )(ta, tg, sa, sg, pin, pout)


def gradient_kernel(own, other, tseg, tmask, sseg, smask, out):
    rin = 32
    full = own[...] + other[...]
    both, feats = full.shape
    width = out.shape[1]
    rout = width // rin
    row = lax.broadcasted_iota(jnp.int32, (feats, width), 0)
    col = lax.broadcasted_iota(jnp.int32, (feats, width), 1)
    spread_x = (row == col // rout).astype(BF16)
    spread_g = (row - rin == col[:, :] % rout).astype(BF16)
    parts = split(full)
    xrep = sum(mm(part, spread_x, NN) for part in parts[::-1])
    grep = sum(mm(part, spread_g[:, :128], NN) for part in parts[::-1])
    tokens = tseg.shape[1]
    test_row = EX_DEV + TEX_DEV * lax.rem(lax.axis_index("test"), 2)
    label = jnp.concatenate([tseg[...], sseg[...] + test_row], axis=1)
    keep = jnp.concatenate([tmask[...], smask[...]], axis=1)
    ex = lax.broadcasted_iota(jnp.int32, (ROWS, both), 0)
    weight = jnp.where(ex == label, keep, 0).astype(F32).astype(BF16)
    for start in range(0, width, 128):
        outer = xrep[:, start : start + 128] * grep
        out[:, start : start + 128] = sum(mm(weight, part, NN) for part in split(outer)[::-1])


def gradients(own, other, tseg, tmask, sseg, smask):
    return pl.pallas_call(
        gradient_kernel,
        out_shape=jax.ShapeDtypeStruct((ROWS, 1024), F32),
        in_specs=[VMEM] * 6,
        out_specs=VMEM,
        compiler_params=pltpu.CompilerParams(vmem_limit_bytes=16 << 20),
        name="gradients",
    )(own, other, tseg, tmask, sseg, smask)


def score_kernel(peers, near, own, *refs):
    mine = refs[:near]
    theirs = refs[near : 2 * near]
    out, train, test = refs[2 * near :]
    shard, core = lax.axis_index(("train", "test")), lax.axis_index("proj")
    shards = peers + 1

    def put(block, mask):
        slot = lax.rem(mask + shards - 1, shards)
        train[pl.ds(pl.multiple_of(slot * EX_DEV, EX_DEV), EX_DEV), :] = block[:EX_DEV, :]
        test[lax.bitwise_xor(shard, mask)] = block[EX_DEV:, :]

    for k in range(near):
        mask = jnp.where(core == 0, k + 1, (near + k + 1) % shards)
        put(mine[k], mask)
        put(theirs[k], jnp.where(core == 0, (near + k + 1) % shards, k + 1))
    put(own, 0)

    half = shards // 2
    pairs = [test[core * half + n] + test[core * half + n + 1] for n in range(0, half, 2)]
    rows = shards * EX_DEV
    tests = half * TEX_DEV
    x = jnp.concatenate([train[...]] + pairs, axis=0)
    hi, mid, _ = split(x)
    gram = mm(hi[:rows], hi, NT) + (mm(hi[:rows], mid, NT) + mm(mid[:rows], hi, NT))
    lane = lax.broadcasted_iota(jnp.int32, gram.shape, 1)
    line = lax.broadcasted_iota(jnp.int32, gram.shape, 0)
    gram = gram * (1.0 / rows) + jnp.where(lane == line, 1.0, 0.0)
    block = [gram[n * 8 : n * 8 + 8] for n in range(shards)]
    sub = lax.broadcasted_iota(jnp.int32, (8, 1), 0)
    for b in range(shards):
        for j in range(8):
            k = b * 8 + j
            pivot = block[b][j : j + 1, :]
            scaled = pivot / pivot[:, k : k + 1]
            for n in range(b, shards):
                col = block[n][:, k : k + 1]
                if n == b:
                    if b == shards - 1:
                        col = jnp.where(sub == j, 0.0, col)
                    else:
                        col = jnp.where(sub > j, col, 0.0)
                block[n] = block[n] - col * scaled
    last = block[-1]
    diag = jnp.sum(jnp.where(lane[:8] == sub + (rows - 8), last, 0.0), axis=1, keepdims=True)
    out[...] = last[:, rows:] / diag * (rows / 32.0)


def scores(own, mine, theirs, shards):
    near = len(mine)
    return pl.pallas_call(
        functools.partial(score_kernel, shards - 1, near),
        out_shape=jax.ShapeDtypeStruct((EX_DEV, shards * TEX_DEV // 2), F32),
        in_specs=[VMEM] * (1 + 2 * near),
        out_specs=VMEM,
        scratch_shapes=[
            pltpu.VMEM((shards * EX_DEV, 1024), F32),
            pltpu.VMEM((shards, ROWS - EX_DEV, 1024), F32),
        ],
        compiler_params=pltpu.CompilerParams(vmem_limit_bytes=16 << 20),
        name="scores",
    )(own, *mine, *theirs)


def large(own):
    shards = lax.axis_size(("train", "test"))
    total = EX_DEV * shards
    everyone = lax.all_gather(own, ("train", "test"), axis=0)
    width = own.shape[1]
    train_full = everyone[:, :EX_DEV].reshape(total, width)
    tests = everyone[:, EX_DEV : EX_DEV + TEX_DEV] + everyone[:, EX_DEV + TEX_DEV :]
    tests = tests.reshape(TEX_DEV * shards, width)
    cols = TEX_DEV * shards // lax.axis_size("proj")
    test_half = lax.dynamic_slice_in_dim(tests, lax.axis_index("proj") * cols, cols, 0)
    gram = jnp.dot(train_full, train_full.T, precision=lax.Precision.HIGHEST)
    cross = jnp.dot(train_full, test_half.T, precision=lax.Precision.HIGHEST)
    system = gram / total + jnp.eye(total, dtype=F32)
    factor = jnp.linalg.cholesky(system)
    solved = jax.scipy.linalg.cho_solve((factor, True), cross)
    row = lax.axis_index(("train", "test")) * EX_DEV
    return lax.dynamic_slice_in_dim(solved, row, EX_DEV, 0) / jnp.sqrt(F32(width))


def body(ta, tg, tseg, tmask, sa, sg, sseg, smask, pin, pout):
    shards = lax.axis_size(("train", "test"))
    part = project(ta[0], tg[0], sa[0], sg[0], pin.T, pout.T)
    other = lax.ppermute(part, "proj", [(0, 1), (1, 0)])
    own = gradients(part, other, tseg, tmask, sseg, smask)
    if shards != 8:
        return large(own)
    axes = ("train", "test", "proj")
    mine = []
    for first, second in ((1, 5), (2, 6), (3, 7), (4, 0)):
        route = [(i * 2, (i ^ first) * 2) for i in range(8)]
        if second:
            route += [(i * 2 + 1, (i ^ second) * 2 + 1) for i in range(8)]
        mine.append(lax.ppermute(own, axes, route))
    theirs = [lax.ppermute(x, "proj", [(0, 1), (1, 0)]) for x in mine]
    return scores(own, mine, theirs, shards)


def solution(mesh):
    return jax.shard_map(
        body,
        mesh=mesh,
        in_specs=(
            P(("groups", "train", "test"), None, "proj"),
            P(("groups", "train", "test"), None, "proj"),
            P(("groups", "train", "test"), None),
            P(("groups", "train", "test"), None),
            P(("groups", "train", "test"), None, "proj"),
            P(("groups", "train", "test"), None, "proj"),
            P(("groups", "train", "test"), None),
            P(("groups", "train", "test"), None),
            P("proj", None),
            P("proj", None),
        ),
        out_specs=P(("groups", "train", "test"), "proj"),
        check_vma=False,
    )
```

```python
import functools

import jax
import jax.numpy as jnp
from jax import lax
from jax.experimental import pallas as pl
from jax.experimental.pallas import tpu as pltpu
from jax.sharding import PartitionSpec as P

EX_DEV = 8
TEX_DEV = 4
ROWS = 16
ROUTES = ((4, 0), (3, 7), (2, 6), (1, 5))
F32 = jnp.float32
BF16 = jnp.bfloat16
NT = (((1,), (1,)), ((), ()))
NN = (((1,), (0,)), ((), ()))
VMEM = pl.BlockSpec(memory_space=pltpu.VMEM)
SMEM = pl.BlockSpec(memory_space=pltpu.SMEM)
HBM = pl.BlockSpec(memory_space=pltpu.HBM)


def split(x):
    hi = x.astype(BF16)
    rest = x - hi.astype(F32)
    mid = rest.astype(BF16)
    low = (rest - mid.astype(F32)).astype(BF16)
    return hi, mid, low


def mm(a, b, dims):
    return lax.dot_general(a, b, dims, preferred_element_type=F32)


def chunks_of(total, parts):
    size = total // parts
    return [(n * size, size) for n in range(parts)]


def project_kernel(ta, tg, sa, sg, pin, pout, out, acts, grads, win, wout, sems):
    rows = ta.shape[0]
    both = acts.shape[0]
    copies = []

    def copy(src, dst):
        dma = pltpu.make_async_copy(src, dst, sems.at[len(copies)])
        dma.start()
        copies.append(dma)
        return dma

    first = [
        copy(pin, win),
        copy(ta, acts.at[pl.ds(0, rows)]),
        copy(sa, acts.at[pl.ds(rows, both - rows)]),
        copy(pout, wout),
    ]
    later = []
    for start, size in chunks_of(grads.shape[1], 4):
        cols = pl.ds(start, size)
        later.append(
            (
                copy(tg.at[:, cols], grads.at[pl.ds(0, rows), cols]),
                copy(sg.at[:, cols], grads.at[pl.ds(rows, both - rows), cols]),
                start,
                size,
            )
        )
    for dma in first[:3]:
        dma.wait()
    xp = mm(acts[...], win[...], NT)
    first[3].wait()
    gp = None
    for one, two, start, size in later:
        one.wait()
        two.wait()
        cols = slice(start, start + size)
        part = mm(grads[:, cols], wout[:, cols], NT)
        gp = part if gp is None else gp + part
    rin = xp.shape[1]
    out[:, :rin] = xp
    out[:, rin:] = gp


def project(ta, tg, sa, sg, pin, pout):
    both = ta.shape[0] + sa.shape[0]
    rin, rout = pin.shape[0], pout.shape[0]
    return pl.pallas_call(
        project_kernel,
        out_shape=pltpu.VMEM((both, rin + rout), F32),
        in_specs=[HBM] * 6,
        out_specs=VMEM,
        scratch_shapes=[
            pltpu.VMEM((both, ta.shape[1]), BF16),
            pltpu.VMEM((both, tg.shape[1]), BF16),
            pltpu.VMEM(pin.shape, BF16),
            pltpu.VMEM(pout.shape, BF16),
            pltpu.SemaphoreType.DMA((12,)),
        ],
        compiler_params=pltpu.CompilerParams(vmem_limit_bytes=60 << 20),
        name="project",
    )(ta, tg, sa, sg, pin, pout)


def gradient_kernel(own, other, tseg, tmask, sseg, smask, out):
    rin = 32
    full = own[...] + other[...]
    both, feats = full.shape
    width = out.shape[1]
    rout = width // rin
    row = lax.broadcasted_iota(jnp.int32, (feats, width), 0)
    col = lax.broadcasted_iota(jnp.int32, (feats, width), 1)
    spread_x = (row == col // rout).astype(BF16)
    spread_g = (row - rin == col[:, :] % rout).astype(BF16)
    parts = split(full)
    xrep = sum(mm(part, spread_x, NN) for part in parts[::-1])
    grep = sum(mm(part, spread_g[:, :128], NN) for part in parts[::-1])
    tokens = tseg.shape[1]
    test_row = EX_DEV + TEX_DEV * lax.rem(lax.axis_index("test"), 2)
    label = jnp.concatenate([tseg[...], sseg[...] + test_row], axis=1)
    keep = jnp.concatenate([tmask[...], smask[...]], axis=1)
    ex = lax.broadcasted_iota(jnp.int32, (ROWS, both), 0)
    weight = jnp.where(ex == label, keep, 0).astype(F32).astype(BF16)
    for start in range(0, width, 128):
        outer = xrep[:, start : start + 128] * grep
        out[:, start : start + 128] = sum(mm(weight, part, NN) for part in split(outer)[::-1])


def gradients(own, other, tseg, tmask, sseg, smask):
    return pl.pallas_call(
        gradient_kernel,
        out_shape=jax.ShapeDtypeStruct((ROWS, 1024), F32),
        in_specs=[VMEM] * 6,
        out_specs=VMEM,
        compiler_params=pltpu.CompilerParams(vmem_limit_bytes=16 << 20),
        name="gradients",
    )(own, other, tseg, tmask, sseg, smask)


def score_kernel(routes, shards, own, *refs):
    near = len(routes)
    mine = refs[:near]
    theirs = refs[near : 2 * near]
    out, train, test = refs[2 * near :]
    shard, core = lax.axis_index(("train", "test")), lax.axis_index("proj")

    def put(block, mask):
        slot = lax.rem(mask + shards - 1, shards)
        train[pl.ds(pl.multiple_of(slot * EX_DEV, EX_DEV), EX_DEV), :] = block[:EX_DEV, :]
        test[lax.bitwise_xor(shard, mask)] = block[EX_DEV:, :]

    for k, (first, second) in enumerate(routes):
        put(mine[k], jnp.where(core == 0, first, second))
        put(theirs[k], jnp.where(core == 0, second, first))
    put(own, 0)

    half = shards // 2
    pairs = [test[core * half + n] + test[core * half + n + 1] for n in range(0, half, 2)]
    rows = shards * EX_DEV
    tests = half * TEX_DEV
    x = jnp.concatenate([train[...]] + pairs, axis=0)
    hi, mid, _ = split(x)
    gram = mm(hi[:rows], hi, NT) + (mm(hi[:rows], mid, NT) + mm(mid[:rows], hi, NT))
    lane = lax.broadcasted_iota(jnp.int32, gram.shape, 1)
    line = lax.broadcasted_iota(jnp.int32, gram.shape, 0)
    gram = gram * (1.0 / rows) + jnp.where(lane == line, 1.0, 0.0)
    block = [gram[n * 8 : n * 8 + 8] for n in range(shards)]
    sub = lax.broadcasted_iota(jnp.int32, (8, 1), 0)
    for b in range(shards):
        for j in range(8):
            k = b * 8 + j
            pivot = block[b][j : j + 1, :]
            scaled = pivot / pivot[:, k : k + 1]
            for n in range(b, shards):
                col = block[n][:, k : k + 1]
                if n == b:
                    if b == shards - 1:
                        col = jnp.where(sub == j, 0.0, col)
                    else:
                        col = jnp.where(sub > j, col, 0.0)
                block[n] = block[n] - col * scaled
    last = block[-1]
    diag = jnp.sum(jnp.where(lane[:8] == sub + (rows - 8), last, 0.0), axis=1, keepdims=True)
    out[...] = last[:, rows:] / diag * (rows / 32.0)


def scores(own, mine, theirs, routes, shards):
    near = len(mine)
    return pl.pallas_call(
        functools.partial(score_kernel, routes, shards),
        out_shape=jax.ShapeDtypeStruct((EX_DEV, shards * TEX_DEV // 2), F32),
        in_specs=[VMEM] * (1 + 2 * near),
        out_specs=VMEM,
        scratch_shapes=[
            pltpu.VMEM((shards * EX_DEV, 1024), F32),
            pltpu.VMEM((shards, ROWS - EX_DEV, 1024), F32),
        ],
        compiler_params=pltpu.CompilerParams(vmem_limit_bytes=16 << 20),
        name="scores",
    )(own, *mine, *theirs)


def large(own):
    shards = lax.axis_size(("train", "test"))
    total = EX_DEV * shards
    everyone = lax.all_gather(own, ("train", "test"), axis=0)
    width = own.shape[1]
    train_full = everyone[:, :EX_DEV].reshape(total, width)
    tests = everyone[:, EX_DEV : EX_DEV + TEX_DEV] + everyone[:, EX_DEV + TEX_DEV :]
    tests = tests.reshape(TEX_DEV * shards, width)
    cols = TEX_DEV * shards // lax.axis_size("proj")
    test_half = lax.dynamic_slice_in_dim(tests, lax.axis_index("proj") * cols, cols, 0)
    gram = jnp.dot(train_full, train_full.T, precision=lax.Precision.HIGHEST)
    cross = jnp.dot(train_full, test_half.T, precision=lax.Precision.HIGHEST)
    system = gram / total + jnp.eye(total, dtype=F32)
    factor = jnp.linalg.cholesky(system)
    solved = jax.scipy.linalg.cho_solve((factor, True), cross)
    row = lax.axis_index(("train", "test")) * EX_DEV
    return lax.dynamic_slice_in_dim(solved, row, EX_DEV, 0) / jnp.sqrt(F32(width))


def body(ta, tg, tseg, tmask, sa, sg, sseg, smask, pin, pout):
    shards = lax.axis_size(("train", "test"))
    part = project(ta[0], tg[0], sa[0], sg[0], pin.T, pout.T)
    other = lax.ppermute(part, "proj", [(0, 1), (1, 0)])
    own = gradients(part, other, tseg, tmask, sseg, smask)
    if shards != 8:
        return large(own)
    axes = ("train", "test", "proj")
    mine = []
    for pair in ROUTES:
        route = [(2 * i + c, 2 * (i ^ pair[c]) + c) for c in range(2) if pair[c] for i in range(shards)]
        mine.append(lax.ppermute(own, axes, route))
    theirs = [lax.ppermute(x, "proj", [(0, 1), (1, 0)]) for x in mine]
    return scores(own, mine, theirs, ROUTES, shards)


def solution(mesh):
    return jax.shard_map(
        body,
        mesh=mesh,
        in_specs=(
            P(("groups", "train", "test"), None, "proj"),
            P(("groups", "train", "test"), None, "proj"),
            P(("groups", "train", "test"), None),
            P(("groups", "train", "test"), None),
            P(("groups", "train", "test"), None, "proj"),
            P(("groups", "train", "test"), None, "proj"),
            P(("groups", "train", "test"), None),
            P(("groups", "train", "test"), None),
            P("proj", None),
            P("proj", None),
        ),
        out_specs=P(("groups", "train", "test"), "proj"),
        check_vma=False,
    )
```

```python
import functools

import jax
import jax.numpy as jnp
from jax import lax
from jax.experimental import pallas as pl
from jax.experimental.pallas import tpu as pltpu
from jax.sharding import PartitionSpec as P

EX_DEV = 8
TEX_DEV = 4
ROWS = 16
ROUTES = ((4, 0), (3, 7), (2, 6), (1, 5))
F32 = jnp.float32
BF16 = jnp.bfloat16
NT = (((1,), (1,)), ((), ()))
NN = (((1,), (0,)), ((), ()))
VMEM = pl.BlockSpec(memory_space=pltpu.VMEM)
SMEM = pl.BlockSpec(memory_space=pltpu.SMEM)
HBM = pl.BlockSpec(memory_space=pltpu.HBM)


def split(x):
    hi = x.astype(BF16)
    rest = x - hi.astype(F32)
    mid = rest.astype(BF16)
    low = (rest - mid.astype(F32)).astype(BF16)
    return hi, mid, low


def mm(a, b, dims):
    return lax.dot_general(a, b, dims, preferred_element_type=F32)


def chunks_of(total, parts):
    size = total // parts
    return [(n * size, size) for n in range(parts)]


def project_kernel(ta, tg, sa, sg, pin, pout, out, acts, grads, win, wout, sems):
    rows = ta.shape[0]
    both = acts.shape[0]
    copies = []

    def copy(src, dst):
        dma = pltpu.make_async_copy(src, dst, sems.at[len(copies)])
        dma.start()
        copies.append(dma)
        return dma

    first = [
        copy(pin, win),
        copy(ta, acts.at[pl.ds(0, rows)]),
        copy(sa, acts.at[pl.ds(rows, both - rows)]),
        copy(pout, wout),
    ]
    later = []
    for start, size in chunks_of(grads.shape[1], 4):
        cols = pl.ds(start, size)
        later.append(
            (
                copy(tg.at[:, cols], grads.at[pl.ds(0, rows), cols]),
                copy(sg.at[:, cols], grads.at[pl.ds(rows, both - rows), cols]),
                start,
                size,
            )
        )
    for dma in first[:3]:
        dma.wait()
    xp = mm(acts[...], win[...], NT)
    first[3].wait()
    gp = None
    for one, two, start, size in later:
        one.wait()
        two.wait()
        cols = slice(start, start + size)
        part = mm(grads[:, cols], wout[:, cols], NT)
        gp = part if gp is None else gp + part
    rin = xp.shape[1]
    out[:, :rin] = xp
    out[:, rin:] = gp


def project(ta, tg, sa, sg, pin, pout):
    both = ta.shape[0] + sa.shape[0]
    rin, rout = pin.shape[0], pout.shape[0]
    return pl.pallas_call(
        project_kernel,
        out_shape=pltpu.VMEM((both, rin + rout), F32),
        in_specs=[HBM] * 6,
        out_specs=VMEM,
        scratch_shapes=[
            pltpu.VMEM((both, ta.shape[1]), BF16),
            pltpu.VMEM((both, tg.shape[1]), BF16),
            pltpu.VMEM(pin.shape, BF16),
            pltpu.VMEM(pout.shape, BF16),
            pltpu.SemaphoreType.DMA((12,)),
        ],
        compiler_params=pltpu.CompilerParams(vmem_limit_bytes=60 << 20),
        name="project",
    )(ta, tg, sa, sg, pin, pout)


def gradient_kernel(own, other, tseg, tmask, sseg, smask, out):
    rin = 32
    full = own[...] + other[...]
    both, feats = full.shape
    width = out.shape[1]
    rout = width // rin
    row = lax.broadcasted_iota(jnp.int32, (feats, width), 0)
    col = lax.broadcasted_iota(jnp.int32, (feats, width), 1)
    spread_x = (row == col // rout).astype(BF16)
    spread_g = (row - rin == col[:, :] % rout).astype(BF16)
    parts = split(full)
    xrep = sum(mm(part, spread_x, NN) for part in parts[::-1])
    grep = sum(mm(part, spread_g[:, :128], NN) for part in parts[::-1])
    tokens = tseg.shape[1]
    test_row = EX_DEV + TEX_DEV * lax.rem(lax.axis_index("test"), 2)
    label = jnp.concatenate([tseg[...], sseg[...] + test_row], axis=1)
    keep = jnp.concatenate([tmask[...], smask[...]], axis=1)
    ex = lax.broadcasted_iota(jnp.int32, (ROWS, both), 0)
    weight = jnp.where(ex == label, keep, 0).astype(F32).astype(BF16)
    for start in range(0, width, 128):
        outer = xrep[:, start : start + 128] * grep
        out[:, start : start + 128] = sum(mm(weight, part, NN) for part in split(outer)[::-1])


def gradients(own, other, tseg, tmask, sseg, smask):
    return pl.pallas_call(
        gradient_kernel,
        out_shape=jax.ShapeDtypeStruct((ROWS, 1024), F32),
        in_specs=[VMEM] * 6,
        out_specs=VMEM,
        compiler_params=pltpu.CompilerParams(vmem_limit_bytes=16 << 20),
        name="gradients",
    )(own, other, tseg, tmask, sseg, smask)


def pivot_rows(block, first):
    shape = block.shape
    rows = [jnp.broadcast_to(block[i : i + 1, :], shape) for i in range(8)]
    a = [[jnp.broadcast_to(rows[i][:, first + j : first + j + 1], shape) for j in range(i + 1)] for i in range(8)]
    low = [[None] * 8 for _ in range(8)]
    inverse = []
    for j in range(8):
        inverse.append(1.0 / a[j][j])
        for i in range(j + 1, 8):
            low[i][j] = a[i][j] * inverse[j]
        for i in range(j + 1, 8):
            for m in range(j + 1, i + 1):
                a[i][m] = a[i][m] - low[i][j] * a[m][j]
            rows[i] = rows[i] - low[i][j] * rows[j]
    solved = [None] * 8
    for i in range(7, -1, -1):
        value = rows[i] * inverse[i]
        for j in range(i + 1, 8):
            value = value - low[j][i] * solved[j]
        solved[i] = value
    return solved


def score_kernel(routes, shards, own, *refs):
    near = len(routes)
    mine = refs[:near]
    theirs = refs[near : 2 * near]
    out, train, test = refs[2 * near :]
    shard, core = lax.axis_index(("train", "test")), lax.axis_index("proj")

    def put(block, mask):
        slot = lax.rem(mask + shards - 1, shards)
        train[pl.ds(pl.multiple_of(slot * EX_DEV, EX_DEV), EX_DEV), :] = block[:EX_DEV, :]
        test[lax.bitwise_xor(shard, mask)] = block[EX_DEV:, :]

    for k, (first, second) in enumerate(routes):
        put(mine[k], jnp.where(core == 0, first, second))
        put(theirs[k], jnp.where(core == 0, second, first))
    put(own, 0)

    half = shards // 2
    pairs = [test[core * half + n] + test[core * half + n + 1] for n in range(0, half, 2)]
    rows = shards * EX_DEV
    tests = half * TEX_DEV
    x = jnp.concatenate([train[...]] + pairs, axis=0)
    hi, mid, _ = split(x)
    gram = mm(hi[:rows], hi, NT) + (mm(hi[:rows], mid, NT) + mm(mid[:rows], hi, NT))
    lane = lax.broadcasted_iota(jnp.int32, gram.shape, 1)
    line = lax.broadcasted_iota(jnp.int32, gram.shape, 0)
    gram = gram * (1.0 / rows) + jnp.where(lane == line, 1.0, 0.0)
    block = [gram[n * 8 : n * 8 + 8] for n in range(shards)]
    for b in range(shards):
        weights = pivot_rows(block[b], b * 8)
        for n in range(b + 1, shards):
            left = block[n]
            for j, row in enumerate(weights):
                left = left - block[n][:, b * 8 + j : b * 8 + j + 1] * row
            block[n] = left
    sub = lax.broadcasted_iota(jnp.int32, block[0].shape, 0)
    own_rows = weights[0]
    for i in range(1, 8):
        own_rows = jnp.where(sub == i, weights[i], own_rows)
    out[...] = own_rows[:, rows:] * (rows / 32.0)


def scores(own, mine, theirs, routes, shards):
    near = len(mine)
    return pl.pallas_call(
        functools.partial(score_kernel, routes, shards),
        out_shape=jax.ShapeDtypeStruct((EX_DEV, shards * TEX_DEV // 2), F32),
        in_specs=[VMEM] * (1 + 2 * near),
        out_specs=VMEM,
        scratch_shapes=[
            pltpu.VMEM((shards * EX_DEV, 1024), F32),
            pltpu.VMEM((shards, ROWS - EX_DEV, 1024), F32),
        ],
        compiler_params=pltpu.CompilerParams(vmem_limit_bytes=16 << 20),
        name="scores",
    )(own, *mine, *theirs)


def large(own):
    shards = lax.axis_size(("train", "test"))
    total = EX_DEV * shards
    everyone = lax.all_gather(own, ("train", "test"), axis=0)
    width = own.shape[1]
    train_full = everyone[:, :EX_DEV].reshape(total, width)
    tests = everyone[:, EX_DEV : EX_DEV + TEX_DEV] + everyone[:, EX_DEV + TEX_DEV :]
    tests = tests.reshape(TEX_DEV * shards, width)
    cols = TEX_DEV * shards // lax.axis_size("proj")
    test_half = lax.dynamic_slice_in_dim(tests, lax.axis_index("proj") * cols, cols, 0)
    gram = jnp.dot(train_full, train_full.T, precision=lax.Precision.HIGHEST)
    cross = jnp.dot(train_full, test_half.T, precision=lax.Precision.HIGHEST)
    system = gram / total + jnp.eye(total, dtype=F32)
    factor = jnp.linalg.cholesky(system)
    solved = jax.scipy.linalg.cho_solve((factor, True), cross)
    row = lax.axis_index(("train", "test")) * EX_DEV
    return lax.dynamic_slice_in_dim(solved, row, EX_DEV, 0) / jnp.sqrt(F32(width))


def body(ta, tg, tseg, tmask, sa, sg, sseg, smask, pin, pout):
    shards = lax.axis_size(("train", "test"))
    part = project(ta[0], tg[0], sa[0], sg[0], pin.T, pout.T)
    other = lax.ppermute(part, "proj", [(0, 1), (1, 0)])
    own = gradients(part, other, tseg, tmask, sseg, smask)
    if shards != 8:
        return large(own)
    axes = ("train", "test", "proj")
    mine = []
    for pair in ROUTES:
        route = [(2 * i + c, 2 * (i ^ pair[c]) + c) for c in range(2) if pair[c] for i in range(shards)]
        mine.append(lax.ppermute(own, axes, route))
    theirs = [lax.ppermute(x, "proj", [(0, 1), (1, 0)]) for x in mine]
    return scores(own, mine, theirs, ROUTES, shards)


def solution(mesh):
    return jax.shard_map(
        body,
        mesh=mesh,
        in_specs=(
            P(("groups", "train", "test"), None, "proj"),
            P(("groups", "train", "test"), None, "proj"),
            P(("groups", "train", "test"), None),
            P(("groups", "train", "test"), None),
            P(("groups", "train", "test"), None, "proj"),
            P(("groups", "train", "test"), None, "proj"),
            P(("groups", "train", "test"), None),
            P(("groups", "train", "test"), None),
            P("proj", None),
            P("proj", None),
        ),
        out_specs=P(("groups", "train", "test"), "proj"),
        check_vma=False,
    )
```

```python
import functools

import jax
import jax.numpy as jnp
from jax import lax
from jax.experimental import pallas as pl
from jax.experimental.pallas import tpu as pltpu
from jax.sharding import PartitionSpec as P

EX_DEV = 8
TEX_DEV = 4
ROWS = 16
ROUTES = ((4, 0), (1, 5), (2, 6), (3, 7))
F32 = jnp.float32
BF16 = jnp.bfloat16
NT = (((1,), (1,)), ((), ()))
NN = (((1,), (0,)), ((), ()))
VMEM = pl.BlockSpec(memory_space=pltpu.VMEM)
SMEM = pl.BlockSpec(memory_space=pltpu.SMEM)
HBM = pl.BlockSpec(memory_space=pltpu.HBM)


def split(x):
    hi = x.astype(BF16)
    rest = x - hi.astype(F32)
    mid = rest.astype(BF16)
    low = (rest - mid.astype(F32)).astype(BF16)
    return hi, mid, low


def mm(a, b, dims):
    return lax.dot_general(a, b, dims, preferred_element_type=F32)


def chunks_of(total, parts):
    size = total // parts
    return [(n * size, size) for n in range(parts)]


def project_kernel(ta, tg, sa, sg, pin, pout, out, acts, grads, win, wout, sems):
    rows = ta.shape[0]
    both = acts.shape[0]
    copies = []

    def copy(src, dst):
        dma = pltpu.make_async_copy(src, dst, sems.at[len(copies)])
        dma.start()
        copies.append(dma)
        return dma

    first = [
        copy(pin, win),
        copy(ta, acts.at[pl.ds(0, rows)]),
        copy(sa, acts.at[pl.ds(rows, both - rows)]),
        copy(pout, wout),
    ]
    later = []
    for start, size in chunks_of(grads.shape[1], 4):
        cols = pl.ds(start, size)
        later.append(
            (
                copy(tg.at[:, cols], grads.at[pl.ds(0, rows), cols]),
                copy(sg.at[:, cols], grads.at[pl.ds(rows, both - rows), cols]),
                start,
                size,
            )
        )
    for dma in first[:3]:
        dma.wait()
    xp = mm(acts[...], win[...], NT)
    first[3].wait()
    gp = None
    for one, two, start, size in later:
        one.wait()
        two.wait()
        cols = slice(start, start + size)
        part = mm(grads[:, cols], wout[:, cols], NT)
        gp = part if gp is None else gp + part
    rin = xp.shape[1]
    out[:, :rin] = xp
    out[:, rin:] = gp


def project(ta, tg, sa, sg, pin, pout):
    both = ta.shape[0] + sa.shape[0]
    rin, rout = pin.shape[0], pout.shape[0]
    return pl.pallas_call(
        project_kernel,
        out_shape=pltpu.VMEM((both, rin + rout), F32),
        in_specs=[HBM] * 6,
        out_specs=VMEM,
        scratch_shapes=[
            pltpu.VMEM((both, ta.shape[1]), BF16),
            pltpu.VMEM((both, tg.shape[1]), BF16),
            pltpu.VMEM(pin.shape, BF16),
            pltpu.VMEM(pout.shape, BF16),
            pltpu.SemaphoreType.DMA((12,)),
        ],
        compiler_params=pltpu.CompilerParams(vmem_limit_bytes=60 << 20),
        name="project",
    )(ta, tg, sa, sg, pin, pout)


def gradient_kernel(own, other, tseg, tmask, sseg, smask, out):
    rin = 32
    full = own[...] + other[...]
    both, feats = full.shape
    width = out.shape[1]
    rout = width // rin
    row = lax.broadcasted_iota(jnp.int32, (feats, width), 0)
    col = lax.broadcasted_iota(jnp.int32, (feats, width), 1)
    spread_x = (row == col // rout).astype(BF16)
    spread_g = (row - rin == col[:, :] % rout).astype(BF16)
    parts = split(full)
    xrep = sum(mm(part, spread_x, NN) for part in parts[::-1])
    grep = sum(mm(part, spread_g[:, :128], NN) for part in parts[::-1])
    tokens = tseg.shape[1]
    test_row = EX_DEV + TEX_DEV * lax.rem(lax.axis_index("test"), 2)
    label = jnp.concatenate([tseg[...], sseg[...] + test_row], axis=1)
    keep = jnp.concatenate([tmask[...], smask[...]], axis=1)
    ex = lax.broadcasted_iota(jnp.int32, (ROWS, both), 0)
    weight = jnp.where(ex == label, keep, 0).astype(F32).astype(BF16)
    for start in range(0, width, 128):
        outer = xrep[:, start : start + 128] * grep
        out[:, start : start + 128] = sum(mm(weight, part, NN) for part in split(outer)[::-1])


def gradients(own, other, tseg, tmask, sseg, smask):
    return pl.pallas_call(
        gradient_kernel,
        out_shape=jax.ShapeDtypeStruct((ROWS, 1024), F32),
        in_specs=[VMEM] * 6,
        out_specs=VMEM,
        compiler_params=pltpu.CompilerParams(vmem_limit_bytes=16 << 20),
        name="gradients",
    )(own, other, tseg, tmask, sseg, smask)


def pivot_rows(block, first):
    shape = block.shape
    rows = [jnp.broadcast_to(block[i : i + 1, :], shape) for i in range(8)]
    a = [[jnp.broadcast_to(rows[i][:, first + j : first + j + 1], shape) for j in range(i + 1)] for i in range(8)]
    low = [[None] * 8 for _ in range(8)]
    pivots = []
    for j in range(0, 8, 2):
        p, q, r = a[j][j], a[j + 1][j], a[j + 1][j + 1]
        scale = 1.0 / (p * r - q * q)
        p, q, r = r * scale, q * scale, p * scale
        pivots.append((p, q, r))
        for i in range(j + 2, 8):
            low[i][j] = a[i][j] * p - a[i][j + 1] * q
            low[i][j + 1] = a[i][j + 1] * r - a[i][j] * q
        for i in range(j + 2, 8):
            for m in range(j + 2, i + 1):
                a[i][m] = a[i][m] - (low[i][j] * a[m][j] + low[i][j + 1] * a[m][j + 1])
            rows[i] = rows[i] - (low[i][j] * rows[j] + low[i][j + 1] * rows[j + 1])
    solved = [None] * 8
    for j in range(6, -1, -2):
        p, q, r = pivots[j // 2]
        upper = rows[j] * p - rows[j + 1] * q
        lower = rows[j + 1] * r - rows[j] * q
        for i in range(j + 2, 8):
            upper = upper - low[i][j] * solved[i]
            lower = lower - low[i][j + 1] * solved[i]
        solved[j], solved[j + 1] = upper, lower
    return solved


def score_kernel(routes, shards, own, *refs):
    near = len(routes)
    mine = refs[:near]
    theirs = refs[near : 2 * near]
    out, train, test = refs[2 * near :]
    shard, core = lax.axis_index(("train", "test")), lax.axis_index("proj")

    def put(block, mask):
        slot = lax.rem(mask + shards - 1, shards)
        train[pl.ds(pl.multiple_of(slot * EX_DEV, EX_DEV), EX_DEV), :] = block[:EX_DEV, :]
        test[lax.bitwise_xor(shard, mask)] = block[EX_DEV:, :]

    for k, (first, second) in enumerate(routes):
        put(mine[k], jnp.where(core == 0, first, second))
        put(theirs[k], jnp.where(core == 0, second, first))
    put(own, 0)

    half = shards // 2
    pairs = [test[core * half + n] + test[core * half + n + 1] for n in range(0, half, 2)]
    rows = shards * EX_DEV
    tests = half * TEX_DEV
    x = jnp.concatenate([train[...]] + pairs, axis=0)
    hi, mid, _ = split(x)
    gram = mm(hi[:rows], hi, NT) + (mm(hi[:rows], mid, NT) + mm(mid[:rows], hi, NT))
    lane = lax.broadcasted_iota(jnp.int32, gram.shape, 1)
    line = lax.broadcasted_iota(jnp.int32, gram.shape, 0)
    gram = gram * (1.0 / rows) + jnp.where(lane == line, 1.0, 0.0)
    block = [gram[n * 8 : n * 8 + 8] for n in range(shards)]
    for b in range(shards):
        weights = pivot_rows(block[b], b * 8)
        for n in range(b + 1, shards):
            left = block[n]
            for j, row in enumerate(weights):
                left = left - block[n][:, b * 8 + j : b * 8 + j + 1] * row
            block[n] = left
    sub = lax.broadcasted_iota(jnp.int32, block[0].shape, 0)
    own_rows = weights[0]
    for i in range(1, 8):
        own_rows = jnp.where(sub == i, weights[i], own_rows)
    out[...] = own_rows[:, rows:] * (rows / 32.0)


def scores(own, mine, theirs, routes, shards):
    near = len(mine)
    return pl.pallas_call(
        functools.partial(score_kernel, routes, shards),
        out_shape=jax.ShapeDtypeStruct((EX_DEV, shards * TEX_DEV // 2), F32),
        in_specs=[VMEM] * (1 + 2 * near),
        out_specs=VMEM,
        scratch_shapes=[
            pltpu.VMEM((shards * EX_DEV, 1024), F32),
            pltpu.VMEM((shards, ROWS - EX_DEV, 1024), F32),
        ],
        compiler_params=pltpu.CompilerParams(vmem_limit_bytes=16 << 20),
        name="scores",
    )(own, *mine, *theirs)


def large(own):
    shards = lax.axis_size(("train", "test"))
    total = EX_DEV * shards
    everyone = lax.all_gather(own, ("train", "test"), axis=0)
    width = own.shape[1]
    train_full = everyone[:, :EX_DEV].reshape(total, width)
    tests = everyone[:, EX_DEV : EX_DEV + TEX_DEV] + everyone[:, EX_DEV + TEX_DEV :]
    tests = tests.reshape(TEX_DEV * shards, width)
    cols = TEX_DEV * shards // lax.axis_size("proj")
    test_half = lax.dynamic_slice_in_dim(tests, lax.axis_index("proj") * cols, cols, 0)
    gram = jnp.dot(train_full, train_full.T, precision=lax.Precision.HIGHEST)
    cross = jnp.dot(train_full, test_half.T, precision=lax.Precision.HIGHEST)
    system = gram / total + jnp.eye(total, dtype=F32)
    factor = jnp.linalg.cholesky(system)
    solved = jax.scipy.linalg.cho_solve((factor, True), cross)
    row = lax.axis_index(("train", "test")) * EX_DEV
    return lax.dynamic_slice_in_dim(solved, row, EX_DEV, 0) / jnp.sqrt(F32(width))


def body(ta, tg, tseg, tmask, sa, sg, sseg, smask, pin, pout):
    shards = lax.axis_size(("train", "test"))
    part = project(ta[0], tg[0], sa[0], sg[0], pin.T, pout.T)
    other = lax.ppermute(part, "proj", [(0, 1), (1, 0)])
    own = gradients(part, other, tseg, tmask, sseg, smask)
    if shards != 8:
        return large(own)
    axes = ("train", "test", "proj")
    mine = []
    for pair in ROUTES:
        route = [(2 * i + c, 2 * (i ^ pair[c]) + c) for c in range(2) if pair[c] for i in range(shards)]
        mine.append(lax.ppermute(own, axes, route))
    theirs = [lax.ppermute(x, "proj", [(0, 1), (1, 0)]) for x in mine]
    return scores(own, mine, theirs, ROUTES, shards)


def solution(mesh):
    return jax.shard_map(
        body,
        mesh=mesh,
        in_specs=(
            P(("groups", "train", "test"), None, "proj"),
            P(("groups", "train", "test"), None, "proj"),
            P(("groups", "train", "test"), None),
            P(("groups", "train", "test"), None),
            P(("groups", "train", "test"), None, "proj"),
            P(("groups", "train", "test"), None, "proj"),
            P(("groups", "train", "test"), None),
            P(("groups", "train", "test"), None),
            P("proj", None),
            P("proj", None),
        ),
        out_specs=P(("groups", "train", "test"), "proj"),
        check_vma=False,
    )
```

```python
import functools

import jax
import jax.numpy as jnp
from jax import lax
from jax.experimental import pallas as pl
from jax.experimental.pallas import tpu as pltpu
from jax.sharding import PartitionSpec as P

EX_DEV = 8
TEX_DEV = 4
ROWS = 16
ROUTES = ((4, 0), (1, 5), (2, 6), (3, 7))
F32 = jnp.float32
BF16 = jnp.bfloat16
NT = (((1,), (1,)), ((), ()))
NN = (((1,), (0,)), ((), ()))
VMEM = pl.BlockSpec(memory_space=pltpu.VMEM)
SMEM = pl.BlockSpec(memory_space=pltpu.SMEM)
HBM = pl.BlockSpec(memory_space=pltpu.HBM)


def split(x):
    hi = x.astype(BF16)
    rest = x - hi.astype(F32)
    mid = rest.astype(BF16)
    low = (rest - mid.astype(F32)).astype(BF16)
    return hi, mid, low


def mm(a, b, dims):
    return lax.dot_general(a, b, dims, preferred_element_type=F32)


def chunks_of(total, parts):
    size = total // parts
    return [(n * size, size) for n in range(parts)]


def project_kernel(ta, tg, sa, sg, pin, pout, out, acts, grads, win, wout, sems):
    rows = ta.shape[0]
    both = acts.shape[0]
    copies = []

    def copy(src, dst):
        dma = pltpu.make_async_copy(src, dst, sems.at[len(copies)])
        dma.start()
        copies.append(dma)
        return dma

    first = [
        copy(pin, win),
        copy(ta, acts.at[pl.ds(0, rows)]),
        copy(sa, acts.at[pl.ds(rows, both - rows)]),
        copy(pout, wout),
    ]
    later = []
    for start, size in chunks_of(grads.shape[1], 4):
        cols = pl.ds(start, size)
        later.append(
            (
                copy(tg.at[:, cols], grads.at[pl.ds(0, rows), cols]),
                copy(sg.at[:, cols], grads.at[pl.ds(rows, both - rows), cols]),
                start,
                size,
            )
        )
    for dma in first[:3]:
        dma.wait()
    xp = mm(acts[...], win[...], NT)
    first[3].wait()
    gp = None
    for one, two, start, size in later:
        one.wait()
        two.wait()
        cols = slice(start, start + size)
        part = mm(grads[:, cols], wout[:, cols], NT)
        gp = part if gp is None else gp + part
    rin = xp.shape[1]
    out[:, :rin] = xp
    out[:, rin:] = gp


def project(ta, tg, sa, sg, pin, pout):
    both = ta.shape[0] + sa.shape[0]
    rin, rout = pin.shape[0], pout.shape[0]
    return pl.pallas_call(
        project_kernel,
        out_shape=pltpu.VMEM((both, rin + rout), F32),
        in_specs=[HBM] * 6,
        out_specs=VMEM,
        scratch_shapes=[
            pltpu.VMEM((both, ta.shape[1]), BF16),
            pltpu.VMEM((both, tg.shape[1]), BF16),
            pltpu.VMEM(pin.shape, BF16),
            pltpu.VMEM(pout.shape, BF16),
            pltpu.SemaphoreType.DMA((12,)),
        ],
        compiler_params=pltpu.CompilerParams(vmem_limit_bytes=60 << 20),
        name="project",
    )(ta, tg, sa, sg, pin, pout)


def gradient_kernel(own, other, tseg, tmask, sseg, smask, out):
    rin = 32
    full = own[...] + other[...]
    both, feats = full.shape
    rout = feats - rin
    width = rin * rout
    row = lax.broadcasted_iota(jnp.int32, (feats, width), 0)
    col = lax.broadcasted_iota(jnp.int32, (feats, width), 1)
    spread_x = (row == col // rout).astype(BF16)
    spread_g = (row - rin == col[:, :] % rout).astype(BF16)
    parts = split(full)
    xrep = sum(mm(part, spread_x, NN) for part in parts[::-1])
    grep = sum(mm(part, spread_g[:, :128], NN) for part in parts[::-1])
    tokens = tseg.shape[1]
    keep = jnp.concatenate([tmask[...], smask[...]], axis=1)
    ex = lax.broadcasted_iota(jnp.int32, (ROWS, both), 0)
    weights = []
    for side in range(2):
        label = jnp.concatenate([tseg[...], sseg[...] + (EX_DEV + TEX_DEV * side)], axis=1)
        weights.append(jnp.where(ex == label, keep, 0).astype(F32).astype(BF16))
    half = width // 2
    upper = {}
    for start in range(0, width, 128):
        outer = xrep[:, start : start + 128] * grep
        side, place = divmod(start, half)
        total = sum(mm(weights[side], part, NN) for part in split(outer)[::-1])
        out[:, start : start + 128] = total[:EX_DEV]
        if side == 0:
            upper[place] = total[EX_DEV:]
        else:
            out[:, width + place : width + place + 128] = upper[place] + total[EX_DEV:]


def gradients(own, other, tseg, tmask, sseg, smask):
    return pl.pallas_call(
        gradient_kernel,
        out_shape=jax.ShapeDtypeStruct((EX_DEV, 1536), F32),
        in_specs=[VMEM] * 6,
        out_specs=VMEM,
        compiler_params=pltpu.CompilerParams(vmem_limit_bytes=16 << 20),
        name="gradients",
    )(own, other, tseg, tmask, sseg, smask)


def pivot_rows(block, first):
    shape = block.shape
    rows = [jnp.broadcast_to(block[i : i + 1, :], shape) for i in range(8)]
    a = [[jnp.broadcast_to(rows[i][:, first + j : first + j + 1], shape) for j in range(i + 1)] for i in range(8)]
    low = [[None] * 8 for _ in range(8)]
    pivots = []
    for j in range(0, 8, 2):
        p, q, r = a[j][j], a[j + 1][j], a[j + 1][j + 1]
        scale = 1.0 / (p * r - q * q)
        p, q, r = r * scale, q * scale, p * scale
        pivots.append((p, q, r))
        for i in range(j + 2, 8):
            low[i][j] = a[i][j] * p - a[i][j + 1] * q
            low[i][j + 1] = a[i][j + 1] * r - a[i][j] * q
        for i in range(j + 2, 8):
            for m in range(j + 2, i + 1):
                a[i][m] = a[i][m] - (low[i][j] * a[m][j] + low[i][j + 1] * a[m][j + 1])
            rows[i] = rows[i] - (low[i][j] * rows[j] + low[i][j + 1] * rows[j + 1])
    solved = [None] * 8
    for j in range(6, -1, -2):
        p, q, r = pivots[j // 2]
        upper = rows[j] * p - rows[j + 1] * q
        lower = rows[j + 1] * r - rows[j] * q
        for i in range(j + 2, 8):
            upper = upper - low[i][j] * solved[i]
            lower = lower - low[i][j + 1] * solved[i]
        solved[j], solved[j + 1] = upper, lower
    return solved


def score_kernel(routes, shards, own, *refs):
    near = len(routes)
    mine = refs[:near]
    theirs = refs[near : 2 * near]
    out, train, test = refs[2 * near :]
    shard, core = lax.axis_index(("train", "test")), lax.axis_index("proj")

    def put(block, mask):
        slot = lax.rem(mask + shards - 1, shards)
        train[pl.ds(pl.multiple_of(slot * EX_DEV, EX_DEV), EX_DEV), :] = block[:, :1024]
        test[lax.bitwise_xor(shard, mask)] = block[:, 1024:]

    for k, (first, second) in enumerate(routes):
        put(mine[k], jnp.where(core == 0, first, second))
        put(theirs[k], jnp.where(core == 0, second, first))
    put(own, 0)

    half = shards // 2
    first = lax.broadcasted_iota(jnp.int32, (EX_DEV, 512), 0) < TEX_DEV
    pairs = []
    for n in range(0, half, 2):
        one, two = test[core * half + n], test[core * half + n + 1]
        left = jnp.where(first, one, pltpu.roll(two, TEX_DEV, 0))
        right = jnp.where(first, pltpu.roll(one, TEX_DEV, 0), two)
        pairs.append(jnp.concatenate([left, right], axis=1))
    rows = shards * EX_DEV
    tests = half * TEX_DEV
    x = jnp.concatenate([train[...]] + pairs, axis=0)
    hi, mid, _ = split(x)
    gram = mm(hi[:rows], hi, NT) + (mm(hi[:rows], mid, NT) + mm(mid[:rows], hi, NT))
    lane = lax.broadcasted_iota(jnp.int32, gram.shape, 1)
    line = lax.broadcasted_iota(jnp.int32, gram.shape, 0)
    gram = gram * (1.0 / rows) + jnp.where(lane == line, 1.0, 0.0)
    block = [gram[n * 8 : n * 8 + 8] for n in range(shards)]
    for b in range(shards):
        weights = pivot_rows(block[b], b * 8)
        for n in range(b + 1, shards):
            left = block[n]
            for j, row in enumerate(weights):
                left = left - block[n][:, b * 8 + j : b * 8 + j + 1] * row
            block[n] = left
    sub = lax.broadcasted_iota(jnp.int32, block[0].shape, 0)
    own_rows = weights[0]
    for i in range(1, 8):
        own_rows = jnp.where(sub == i, weights[i], own_rows)
    out[...] = own_rows[:, rows:] * (rows / 32.0)


def scores(own, mine, theirs, routes, shards):
    near = len(mine)
    return pl.pallas_call(
        functools.partial(score_kernel, routes, shards),
        out_shape=jax.ShapeDtypeStruct((EX_DEV, shards * TEX_DEV // 2), F32),
        in_specs=[VMEM] * (1 + 2 * near),
        out_specs=VMEM,
        scratch_shapes=[
            pltpu.VMEM((shards * EX_DEV, 1024), F32),
            pltpu.VMEM((shards, EX_DEV, 512), F32),
        ],
        compiler_params=pltpu.CompilerParams(vmem_limit_bytes=16 << 20),
        name="scores",
    )(own, *mine, *theirs)


def large(own):
    shards = lax.axis_size(("train", "test"))
    total = EX_DEV * shards
    everyone = lax.all_gather(own, ("train", "test"), axis=0)
    width = 2 * own.shape[1] // 3
    train_full = everyone[:, :, :width].reshape(total, width)
    tests = jnp.concatenate([everyone[:, :TEX_DEV, width:], everyone[:, TEX_DEV:, width:]], axis=2)
    tests = tests.reshape(TEX_DEV * shards, width)
    cols = TEX_DEV * shards // lax.axis_size("proj")
    test_half = lax.dynamic_slice_in_dim(tests, lax.axis_index("proj") * cols, cols, 0)
    gram = jnp.dot(train_full, train_full.T, precision=lax.Precision.HIGHEST)
    cross = jnp.dot(train_full, test_half.T, precision=lax.Precision.HIGHEST)
    system = gram / total + jnp.eye(total, dtype=F32)
    factor = jnp.linalg.cholesky(system)
    solved = jax.scipy.linalg.cho_solve((factor, True), cross)
    row = lax.axis_index(("train", "test")) * EX_DEV
    return lax.dynamic_slice_in_dim(solved, row, EX_DEV, 0) / jnp.sqrt(F32(width))


def body(ta, tg, tseg, tmask, sa, sg, sseg, smask, pin, pout):
    shards = lax.axis_size(("train", "test"))
    part = project(ta[0], tg[0], sa[0], sg[0], pin.T, pout.T)
    other = lax.ppermute(part, "proj", [(0, 1), (1, 0)])
    own = gradients(part, other, tseg, tmask, sseg, smask)
    if shards != 8:
        return large(own)
    axes = ("train", "test", "proj")
    mine = []
    for pair in ROUTES:
        route = [(2 * i + c, 2 * (i ^ pair[c]) + c) for c in range(2) if pair[c] for i in range(shards)]
        mine.append(lax.ppermute(own, axes, route))
    theirs = [lax.ppermute(x, "proj", [(0, 1), (1, 0)]) for x in mine]
    return scores(own, mine, theirs, ROUTES, shards)


def solution(mesh):
    return jax.shard_map(
        body,
        mesh=mesh,
        in_specs=(
            P(("groups", "train", "test"), None, "proj"),
            P(("groups", "train", "test"), None, "proj"),
            P(("groups", "train", "test"), None),
            P(("groups", "train", "test"), None),
            P(("groups", "train", "test"), None, "proj"),
            P(("groups", "train", "test"), None, "proj"),
            P(("groups", "train", "test"), None),
            P(("groups", "train", "test"), None),
            P("proj", None),
            P("proj", None),
        ),
        out_specs=P(("groups", "train", "test"), "proj"),
        check_vma=False,
    )
```

```python
import functools

import jax
import jax.numpy as jnp
from jax import lax
from jax.experimental import pallas as pl
from jax.experimental.pallas import tpu as pltpu
from jax.sharding import PartitionSpec as P

EX_DEV = 8
TEX_DEV = 4
ROWS = 16
ROUTES = ((4, 4), (5, 1), (2, 6), (3, 7))
F32 = jnp.float32
BF16 = jnp.bfloat16
NT = (((1,), (1,)), ((), ()))
NN = (((1,), (0,)), ((), ()))
VMEM = pl.BlockSpec(memory_space=pltpu.VMEM)
SMEM = pl.BlockSpec(memory_space=pltpu.SMEM)
HBM = pl.BlockSpec(memory_space=pltpu.HBM)


def split(x):
    hi = x.astype(BF16)
    rest = x - hi.astype(F32)
    mid = rest.astype(BF16)
    low = (rest - mid.astype(F32)).astype(BF16)
    return hi, mid, low


def mm(a, b, dims):
    return lax.dot_general(a, b, dims, preferred_element_type=F32)


def chunks_of(total, parts):
    size = total // parts
    return [(n * size, size) for n in range(parts)]


def project_kernel(ta, tg, sa, sg, pin, pout, out, acts, grads, win, wout, sems):
    rows = ta.shape[0]
    both = acts.shape[0]
    copies = []

    def copy(src, dst):
        dma = pltpu.make_async_copy(src, dst, sems.at[len(copies)])
        dma.start()
        copies.append(dma)
        return dma

    first = [
        copy(pin, win),
        copy(ta, acts.at[pl.ds(0, rows)]),
        copy(sa, acts.at[pl.ds(rows, both - rows)]),
        copy(pout, wout),
    ]
    later = []
    for start, size in chunks_of(grads.shape[1], 4):
        cols = pl.ds(start, size)
        later.append(
            (
                copy(tg.at[:, cols], grads.at[pl.ds(0, rows), cols]),
                copy(sg.at[:, cols], grads.at[pl.ds(rows, both - rows), cols]),
                start,
                size,
            )
        )
    for dma in first[:3]:
        dma.wait()
    xp = mm(acts[...], win[...], NT)
    first[3].wait()
    gp = None
    for one, two, start, size in later:
        one.wait()
        two.wait()
        cols = slice(start, start + size)
        part = mm(grads[:, cols], wout[:, cols], NT)
        gp = part if gp is None else gp + part
    rin = xp.shape[1]
    out[:, :rin] = xp
    out[:, rin:] = gp


def project(ta, tg, sa, sg, pin, pout):
    both = ta.shape[0] + sa.shape[0]
    rin, rout = pin.shape[0], pout.shape[0]
    return pl.pallas_call(
        project_kernel,
        out_shape=pltpu.VMEM((both, rin + rout), F32),
        in_specs=[HBM] * 6,
        out_specs=VMEM,
        scratch_shapes=[
            pltpu.VMEM((both, ta.shape[1]), BF16),
            pltpu.VMEM((both, tg.shape[1]), BF16),
            pltpu.VMEM(pin.shape, BF16),
            pltpu.VMEM(pout.shape, BF16),
            pltpu.SemaphoreType.DMA((12,)),
        ],
        compiler_params=pltpu.CompilerParams(vmem_limit_bytes=60 << 20),
        name="project",
    )(ta, tg, sa, sg, pin, pout)


def gradient_kernel(own, other, tseg, tmask, sseg, smask, out):
    rin = 32
    full = own[...] + other[...]
    both, feats = full.shape
    rout = feats - rin
    width = rin * rout
    row = lax.broadcasted_iota(jnp.int32, (feats, width), 0)
    col = lax.broadcasted_iota(jnp.int32, (feats, width), 1)
    spread_x = (row == col // rout).astype(BF16)
    spread_g = (row - rin == col[:, :] % rout).astype(BF16)
    parts = split(full)
    xrep = sum(mm(part, spread_x, NN) for part in parts[::-1])
    grep = sum(mm(part, spread_g[:, :128], NN) for part in parts[::-1])
    tokens = tseg.shape[1]
    keep = jnp.concatenate([tmask[...], smask[...]], axis=1)
    ex = lax.broadcasted_iota(jnp.int32, (ROWS, both), 0)
    weights = []
    for side in range(2):
        label = jnp.concatenate([tseg[...], sseg[...] + (EX_DEV + TEX_DEV * side)], axis=1)
        weights.append(jnp.where(ex == label, keep, 0).astype(F32).astype(BF16))
    half = width // 2
    upper = {}
    for start in range(0, width, 128):
        outer = xrep[:, start : start + 128] * grep
        side, place = divmod(start, half)
        total = sum(mm(weights[side], part, NN) for part in split(outer)[::-1])
        out[:, start : start + 128] = total[:EX_DEV]
        if side == 0:
            upper[place] = total[EX_DEV:]
        else:
            out[:, width + place : width + place + 128] = upper[place] + total[EX_DEV:]


def gradients(own, other, tseg, tmask, sseg, smask):
    return pl.pallas_call(
        gradient_kernel,
        out_shape=jax.ShapeDtypeStruct((EX_DEV, 1536), F32),
        in_specs=[VMEM] * 6,
        out_specs=VMEM,
        compiler_params=pltpu.CompilerParams(vmem_limit_bytes=16 << 20),
        name="gradients",
    )(own, other, tseg, tmask, sseg, smask)


def pivot_rows(block, first):
    shape = block.shape
    rows = [jnp.broadcast_to(block[i : i + 1, :], shape) for i in range(8)]
    a = [[jnp.broadcast_to(rows[i][:, first + j : first + j + 1], shape) for j in range(i + 1)] for i in range(8)]
    low = [[None] * 8 for _ in range(8)]
    pivots = []
    for j in range(0, 8, 2):
        p, q, r = a[j][j], a[j + 1][j], a[j + 1][j + 1]
        scale = 1.0 / (p * r - q * q)
        p, q, r = r * scale, q * scale, p * scale
        pivots.append((p, q, r))
        for i in range(j + 2, 8):
            low[i][j] = a[i][j] * p - a[i][j + 1] * q
            low[i][j + 1] = a[i][j + 1] * r - a[i][j] * q
        for i in range(j + 2, 8):
            for m in range(j + 2, i + 1):
                a[i][m] = a[i][m] - (low[i][j] * a[m][j] + low[i][j + 1] * a[m][j + 1])
            rows[i] = rows[i] - (low[i][j] * rows[j] + low[i][j + 1] * rows[j + 1])
    solved = [None] * 8
    for j in range(6, -1, -2):
        p, q, r = pivots[j // 2]
        upper = rows[j] * p - rows[j + 1] * q
        lower = rows[j + 1] * r - rows[j] * q
        for i in range(j + 2, 8):
            upper = upper - low[i][j] * solved[i]
            lower = lower - low[i][j + 1] * solved[i]
        solved[j], solved[j + 1] = upper, lower
    return solved


def score_kernel(routes, shards, own, *refs):
    *blocks, out, train, test = refs
    mine = blocks[: len(routes)]
    theirs = iter(blocks[len(routes) :])
    shard, core = lax.axis_index(("train", "test")), lax.axis_index("proj")

    def put(block, mask):
        slot = lax.rem(mask + shards - 1, shards)
        train[pl.ds(pl.multiple_of(slot * EX_DEV, EX_DEV), EX_DEV), :] = block[:, :1024]
        test[lax.bitwise_xor(shard, mask)] = block[:, 1024:]

    for k, (first, second) in enumerate(routes):
        put(mine[k], jnp.where(core == 0, first, second))
        if first != second:
            put(next(theirs), jnp.where(core == 0, second, first))
    put(own, 0)

    half = shards // 2
    first = lax.broadcasted_iota(jnp.int32, (EX_DEV, 512), 0) < TEX_DEV
    pairs = []
    for n in range(0, half, 2):
        one, two = test[core * half + n], test[core * half + n + 1]
        left = jnp.where(first, one, pltpu.roll(two, TEX_DEV, 0))
        right = jnp.where(first, pltpu.roll(one, TEX_DEV, 0), two)
        pairs.append(jnp.concatenate([left, right], axis=1))
    rows = shards * EX_DEV
    tests = half * TEX_DEV
    x = jnp.concatenate([train[...]] + pairs, axis=0)
    hi, mid, _ = split(x)
    gram = mm(hi[:rows], hi, NT) + (mm(hi[:rows], mid, NT) + mm(mid[:rows], hi, NT))
    lane = lax.broadcasted_iota(jnp.int32, gram.shape, 1)
    line = lax.broadcasted_iota(jnp.int32, gram.shape, 0)
    gram = gram * (1.0 / rows) + jnp.where(lane == line, 1.0, 0.0)
    block = [gram[n * 8 : n * 8 + 8] for n in range(shards)]
    for b in range(shards):
        weights = pivot_rows(block[b], b * 8)
        for n in range(b + 1, shards):
            left = block[n]
            for j, row in enumerate(weights):
                left = left - block[n][:, b * 8 + j : b * 8 + j + 1] * row
            block[n] = left
    sub = lax.broadcasted_iota(jnp.int32, block[0].shape, 0)
    own_rows = weights[0]
    for i in range(1, 8):
        own_rows = jnp.where(sub == i, weights[i], own_rows)
    out[...] = own_rows[:, rows:] * (rows / 32.0)


def scores(own, mine, theirs, routes, shards):
    blocks = (own, *mine, *theirs)
    return pl.pallas_call(
        functools.partial(score_kernel, routes, shards),
        out_shape=jax.ShapeDtypeStruct((EX_DEV, shards * TEX_DEV // 2), F32),
        in_specs=[VMEM] * len(blocks),
        out_specs=VMEM,
        scratch_shapes=[
            pltpu.VMEM((shards * EX_DEV, 1024), F32),
            pltpu.VMEM((shards, EX_DEV, 512), F32),
        ],
        compiler_params=pltpu.CompilerParams(vmem_limit_bytes=16 << 20),
        name="scores",
    )(*blocks)


def large(own):
    shards = lax.axis_size(("train", "test"))
    total = EX_DEV * shards
    everyone = lax.all_gather(own, ("train", "test"), axis=0)
    width = 2 * own.shape[1] // 3
    train_full = everyone[:, :, :width].reshape(total, width)
    tests = jnp.concatenate([everyone[:, :TEX_DEV, width:], everyone[:, TEX_DEV:, width:]], axis=2)
    tests = tests.reshape(TEX_DEV * shards, width)
    cols = TEX_DEV * shards // lax.axis_size("proj")
    test_half = lax.dynamic_slice_in_dim(tests, lax.axis_index("proj") * cols, cols, 0)
    gram = jnp.dot(train_full, train_full.T, precision=lax.Precision.HIGHEST)
    cross = jnp.dot(train_full, test_half.T, precision=lax.Precision.HIGHEST)
    system = gram / total + jnp.eye(total, dtype=F32)
    factor = jnp.linalg.cholesky(system)
    solved = jax.scipy.linalg.cho_solve((factor, True), cross)
    row = lax.axis_index(("train", "test")) * EX_DEV
    return lax.dynamic_slice_in_dim(solved, row, EX_DEV, 0) / jnp.sqrt(F32(width))


def body(ta, tg, tseg, tmask, sa, sg, sseg, smask, pin, pout):
    shards = lax.axis_size(("train", "test"))
    part = project(ta[0], tg[0], sa[0], sg[0], pin.T, pout.T)
    other = lax.ppermute(part, "proj", [(0, 1), (1, 0)])
    own = gradients(part, other, tseg, tmask, sseg, smask)
    if shards != 8:
        return large(own)
    axes = ("train", "test", "proj")
    mine = []
    for pair in ROUTES:
        route = [(2 * i + c, 2 * (i ^ pair[c]) + c) for c in range(2) for i in range(shards)]
        mine.append(lax.ppermute(own, axes, route))
    theirs = [lax.ppermute(x, "proj", [(0, 1), (1, 0)]) for x, pair in zip(mine, ROUTES) if pair[0] != pair[1]]
    return scores(own, mine, theirs, ROUTES, shards)


def solution(mesh):
    return jax.shard_map(
        body,
        mesh=mesh,
        in_specs=(
            P(("groups", "train", "test"), None, "proj"),
            P(("groups", "train", "test"), None, "proj"),
            P(("groups", "train", "test"), None),
            P(("groups", "train", "test"), None),
            P(("groups", "train", "test"), None, "proj"),
            P(("groups", "train", "test"), None, "proj"),
            P(("groups", "train", "test"), None),
            P(("groups", "train", "test"), None),
            P("proj", None),
            P("proj", None),
        ),
        out_specs=P(("groups", "train", "test"), "proj"),
        check_vma=False,
    )
```

```python
import functools

import jax
import jax.numpy as jnp
from jax import lax
from jax.experimental import pallas as pl
from jax.experimental.pallas import tpu as pltpu
from jax.sharding import PartitionSpec as P

EX_DEV = 8
TEX_DEV = 4
ROWS = 16
ROUTES = ((4, 4), (5, 1), (2, 6), (3, 7))
F32 = jnp.float32
BF16 = jnp.bfloat16
NT = (((1,), (1,)), ((), ()))
NN = (((1,), (0,)), ((), ()))
VMEM = pl.BlockSpec(memory_space=pltpu.VMEM)
SMEM = pl.BlockSpec(memory_space=pltpu.SMEM)
HBM = pl.BlockSpec(memory_space=pltpu.HBM)


def split(x):
    hi = x.astype(BF16)
    rest = x - hi.astype(F32)
    mid = rest.astype(BF16)
    low = (rest - mid.astype(F32)).astype(BF16)
    return hi, mid, low


def mm(a, b, dims):
    return lax.dot_general(a, b, dims, preferred_element_type=F32)


def chunks_of(total, parts):
    size = total // parts
    return [(n * size, size) for n in range(parts)]


def project_kernel(ta, tg, sa, sg, pin, pout, out, acts, grads, win, wout, sems):
    rows = ta.shape[0]
    both = acts.shape[0]
    copies = []

    def copy(src, dst):
        dma = pltpu.make_async_copy(src, dst, sems.at[len(copies)])
        dma.start()
        copies.append(dma)
        return dma

    first = [
        copy(pin, win),
        copy(ta, acts.at[pl.ds(0, rows)]),
        copy(sa, acts.at[pl.ds(rows, both - rows)]),
        copy(pout, wout),
    ]
    later = []
    for start, size in chunks_of(grads.shape[1], 2):
        cols = pl.ds(start, size)
        later.append(
            (
                copy(tg.at[:, cols], grads.at[pl.ds(0, rows), cols]),
                copy(sg.at[:, cols], grads.at[pl.ds(rows, both - rows), cols]),
                start,
                size,
            )
        )
    for dma in first[:3]:
        dma.wait()
    xp = mm(acts[...], win[...], NT)
    first[3].wait()
    gp = None
    for one, two, start, size in later:
        one.wait()
        two.wait()
        cols = slice(start, start + size)
        part = mm(grads[:, cols], wout[:, cols], NT)
        gp = part if gp is None else gp + part
    rin = xp.shape[1]
    out[:, :rin] = xp
    out[:, rin:] = gp


def project(ta, tg, sa, sg, pin, pout):
    both = ta.shape[0] + sa.shape[0]
    rin, rout = pin.shape[0], pout.shape[0]
    return pl.pallas_call(
        project_kernel,
        out_shape=pltpu.VMEM((both, rin + rout), F32),
        in_specs=[HBM] * 6,
        out_specs=VMEM,
        scratch_shapes=[
            pltpu.VMEM((both, ta.shape[1]), BF16),
            pltpu.VMEM((both, tg.shape[1]), BF16),
            pltpu.VMEM(pin.shape, BF16),
            pltpu.VMEM(pout.shape, BF16),
            pltpu.SemaphoreType.DMA((12,)),
        ],
        compiler_params=pltpu.CompilerParams(vmem_limit_bytes=60 << 20),
        name="project",
    )(ta, tg, sa, sg, pin, pout)


def gradient_kernel(own, other, tseg, tmask, sseg, smask, out):
    rin = 32
    full = own[...] + other[...]
    both, feats = full.shape
    rout = feats - rin
    width = rin * rout
    row = lax.broadcasted_iota(jnp.int32, (feats, width), 0)
    col = lax.broadcasted_iota(jnp.int32, (feats, width), 1)
    spread_x = (row == col // rout).astype(BF16)
    spread_g = (row - rin == col[:, :] % rout).astype(BF16)
    parts = split(full)
    xrep = sum(mm(part, spread_x, NN) for part in parts[1::-1])
    grep = sum(mm(part, spread_g[:, :128], NN) for part in parts[1::-1])
    tokens = tseg.shape[1]
    keep = jnp.concatenate([tmask[...], smask[...]], axis=1)
    ex = lax.broadcasted_iota(jnp.int32, (ROWS, both), 0)
    weights = []
    for side in range(2):
        label = jnp.concatenate([tseg[...], sseg[...] + (EX_DEV + TEX_DEV * side)], axis=1)
        weights.append(jnp.where(ex == label, keep, 0).astype(F32).astype(BF16))
    half = width // 2
    upper = {}
    for start in range(0, width, 128):
        outer = xrep[:, start : start + 128] * grep
        side, place = divmod(start, half)
        total = sum(mm(weights[side], part, NN) for part in split(outer)[1::-1])
        out[:, start : start + 128] = total[:EX_DEV]
        if side == 0:
            upper[place] = total[EX_DEV:]
        else:
            out[:, width + place : width + place + 128] = upper[place] + total[EX_DEV:]


def gradients(own, other, tseg, tmask, sseg, smask):
    return pl.pallas_call(
        gradient_kernel,
        out_shape=jax.ShapeDtypeStruct((EX_DEV, 1536), F32),
        in_specs=[VMEM] * 6,
        out_specs=VMEM,
        compiler_params=pltpu.CompilerParams(vmem_limit_bytes=16 << 20),
        name="gradients",
    )(own, other, tseg, tmask, sseg, smask)


def pivot_rows(block, first):
    shape = block.shape
    rows = [jnp.broadcast_to(block[i : i + 1, :], shape) for i in range(8)]
    a = [[jnp.broadcast_to(rows[i][:, first + j : first + j + 1], shape) for j in range(i + 1)] for i in range(8)]
    low = [[None] * 8 for _ in range(8)]
    pivots = []
    for j in range(0, 8, 2):
        p, q, r = a[j][j], a[j + 1][j], a[j + 1][j + 1]
        scale = 1.0 / (p * r - q * q)
        p, q, r = r * scale, q * scale, p * scale
        pivots.append((p, q, r))
        for i in range(j + 2, 8):
            low[i][j] = a[i][j] * p - a[i][j + 1] * q
            low[i][j + 1] = a[i][j + 1] * r - a[i][j] * q
        for i in range(j + 2, 8):
            for m in range(j + 2, i + 1):
                a[i][m] = a[i][m] - (low[i][j] * a[m][j] + low[i][j + 1] * a[m][j + 1])
            rows[i] = rows[i] - (low[i][j] * rows[j] + low[i][j + 1] * rows[j + 1])
    solved = [None] * 8
    for j in range(6, -1, -2):
        p, q, r = pivots[j // 2]
        upper = rows[j] * p - rows[j + 1] * q
        lower = rows[j + 1] * r - rows[j] * q
        for i in range(j + 2, 8):
            upper = upper - low[i][j] * solved[i]
            lower = lower - low[i][j + 1] * solved[i]
        solved[j], solved[j + 1] = upper, lower
    return solved


def score_kernel(routes, shards, own, *refs):
    *blocks, out, train, test = refs
    mine = blocks[: len(routes)]
    theirs = iter(blocks[len(routes) :])
    shard, core = lax.axis_index(("train", "test")), lax.axis_index("proj")

    def put(block, mask):
        slot = lax.rem(mask + shards - 1, shards)
        train[pl.ds(pl.multiple_of(slot * EX_DEV, EX_DEV), EX_DEV), :] = block[:, :1024]
        test[lax.bitwise_xor(shard, mask)] = block[:, 1024:]

    for k, (first, second) in enumerate(routes):
        put(mine[k], jnp.where(core == 0, first, second))
        if first != second:
            put(next(theirs), jnp.where(core == 0, second, first))
    put(own, 0)

    half = shards // 2
    first = lax.broadcasted_iota(jnp.int32, (EX_DEV, 512), 0) < TEX_DEV
    pairs = []
    for n in range(0, half, 2):
        one, two = test[core * half + n], test[core * half + n + 1]
        left = jnp.where(first, one, pltpu.roll(two, TEX_DEV, 0))
        right = jnp.where(first, pltpu.roll(one, TEX_DEV, 0), two)
        pairs.append(jnp.concatenate([left, right], axis=1))
    rows = shards * EX_DEV
    tests = half * TEX_DEV
    x = jnp.concatenate([train[...]] + pairs, axis=0)
    hi, mid, _ = split(x)
    gram = mm(hi[:rows], hi, NT) + (mm(hi[:rows], mid, NT) + mm(mid[:rows], hi, NT))
    lane = lax.broadcasted_iota(jnp.int32, gram.shape, 1)
    line = lax.broadcasted_iota(jnp.int32, gram.shape, 0)
    gram = gram * (1.0 / rows) + jnp.where(lane == line, 1.0, 0.0)
    block = [gram[n * 8 : n * 8 + 8] for n in range(shards)]
    for b in range(shards):
        weights = pivot_rows(block[b], b * 8)
        for n in range(b + 1, shards):
            left = block[n]
            for j, row in enumerate(weights):
                left = left - block[n][:, b * 8 + j : b * 8 + j + 1] * row
            block[n] = left
    sub = lax.broadcasted_iota(jnp.int32, block[0].shape, 0)
    own_rows = weights[0]
    for i in range(1, 8):
        own_rows = jnp.where(sub == i, weights[i], own_rows)
    out[...] = own_rows[:, rows:] * (rows / 32.0)


def scores(own, mine, theirs, routes, shards):
    blocks = (own, *mine, *theirs)
    return pl.pallas_call(
        functools.partial(score_kernel, routes, shards),
        out_shape=jax.ShapeDtypeStruct((EX_DEV, shards * TEX_DEV // 2), F32),
        in_specs=[VMEM] * len(blocks),
        out_specs=VMEM,
        scratch_shapes=[
            pltpu.VMEM((shards * EX_DEV, 1024), F32),
            pltpu.VMEM((shards, EX_DEV, 512), F32),
        ],
        compiler_params=pltpu.CompilerParams(vmem_limit_bytes=16 << 20),
        name="scores",
    )(*blocks)


def large(own):
    shards = lax.axis_size(("train", "test"))
    total = EX_DEV * shards
    everyone = lax.all_gather(own, ("train", "test"), axis=0)
    width = 2 * own.shape[1] // 3
    train_full = everyone[:, :, :width].reshape(total, width)
    tests = jnp.concatenate([everyone[:, :TEX_DEV, width:], everyone[:, TEX_DEV:, width:]], axis=2)
    tests = tests.reshape(TEX_DEV * shards, width)
    cols = TEX_DEV * shards // lax.axis_size("proj")
    test_half = lax.dynamic_slice_in_dim(tests, lax.axis_index("proj") * cols, cols, 0)
    gram = jnp.dot(train_full, train_full.T, precision=lax.Precision.HIGHEST)
    cross = jnp.dot(train_full, test_half.T, precision=lax.Precision.HIGHEST)
    system = gram / total + jnp.eye(total, dtype=F32)
    factor = jnp.linalg.cholesky(system)
    solved = jax.scipy.linalg.cho_solve((factor, True), cross)
    row = lax.axis_index(("train", "test")) * EX_DEV
    return lax.dynamic_slice_in_dim(solved, row, EX_DEV, 0) / jnp.sqrt(F32(width))


def body(ta, tg, tseg, tmask, sa, sg, sseg, smask, pin, pout):
    shards = lax.axis_size(("train", "test"))
    part = project(ta[0], tg[0], sa[0], sg[0], pin.T, pout.T)
    other = lax.ppermute(part, "proj", [(0, 1), (1, 0)])
    own = gradients(part, other, tseg, tmask, sseg, smask)
    if shards != 8:
        return large(own)
    axes = ("train", "test", "proj")
    mine = []
    for pair in ROUTES:
        route = [(2 * i + c, 2 * (i ^ pair[c]) + c) for c in range(2) for i in range(shards)]
        mine.append(lax.ppermute(own, axes, route))
    theirs = [lax.ppermute(x, "proj", [(0, 1), (1, 0)]) for x, pair in zip(mine, ROUTES) if pair[0] != pair[1]]
    return scores(own, mine, theirs, ROUTES, shards)


def solution(mesh):
    return jax.shard_map(
        body,
        mesh=mesh,
        in_specs=(
            P(("groups", "train", "test"), None, "proj"),
            P(("groups", "train", "test"), None, "proj"),
            P(("groups", "train", "test"), None),
            P(("groups", "train", "test"), None),
            P(("groups", "train", "test"), None, "proj"),
            P(("groups", "train", "test"), None, "proj"),
            P(("groups", "train", "test"), None),
            P(("groups", "train", "test"), None),
            P("proj", None),
            P("proj", None),
        ),
        out_specs=P(("groups", "train", "test"), "proj"),
        check_vma=False,
    )
```
